256 devices in a mesh: col: 4 (over x_hi, core), grp: 64 (over y, x_lo, z).
Axes of the slice: x: 4 (x_hi: 2, x_lo: 2; x = x_hi * 2 + x_lo), y: 4, z: 8, core: 2. Of those that a mesh axis runs over, the one named last changes fastest.
Arguments:
- rows: float32 [4, 32768, 1024], P(None, 'grp', 'col'), may hold values from -6 to 6
- bag_ids: int32 [65536, 4, 16], P('grp'), may hold values from 0 to 511
- bag_lengths: int32 [65536, 4], P('grp'), may hold values from 1 to 16, as said below
- labels: int32 [65536], P('grp'), may hold values 0 or 1
- proj_weight: bfloat16 [4096, 256], replicated, may hold values from -0.09375 to 0.09375
- hidden_weight: bfloat16 [256, 1024], replicated, may hold values from -0.375 to 0.375
- hidden_bias: float32 [1024], replicated, may hold values from -3 to 3
- out_weight: float32 [1024], replicated, may hold values from -0.5 to 0.5
Outputs:
- row_grad: float32 [4, 32768, 1024], P(None, 'grp', 'col')
- proj_grad: float32 [4096, 256], P(('col', 'grp'))
- hidden_grad: float32 [256, 1024], replicated
- bias_grad: float32 [1024], replicated
- out_grad: float32 [1024], replicated
The draws below stay inside these ranges and needn't reach their ends.
Inputs may be any that keep to these rules, and one draw needn't show every extreme that they name: `bag_lengths`: some sample has exactly 16 live lookups in some table.
All inputs are finite; a program needn't handle non-finite values. No bound on the sum of `labels` on one device may be relied on, other than what follows from the above.
Results may differ from the reference program's by a relative error of at most 0.0071.
Values may be sent and summed in bfloat16 or wider, within the bound.
A program may use at most 64 MiB of HBM per device.

```python
import jax
import jax.numpy as jnp
from jax import lax

TABLES = 4
E = 1024
ROWS_DEV = 512
SAMP_GRP = 1024
BAG = 16
PROJ = 256
HID = 1024
SAMPLES = 65536
ROWS = 32768
N_COL = 4
N_GRP = 64


def draw_bag_lengths(key, part):
    key = jax.random.fold_in(key, 7)
    drawn = jax.random.randint(key, (SAMPLES, TABLES), 1, BAG + 1, dtype=jnp.int32)
    return drawn.at[0, 0].set(BAG)


def place_ends(entries, stream_key, smallest, top_value):
    dims = entries.shape
    spot = [jax.random.randint(jax.random.fold_in(stream_key, axis), (), 0, dims[axis]) for axis in range(len(dims))]
    entries = entries.at[tuple(spot)].set(smallest)
    longest = dims.index(max(dims))
    spot[longest] = (spot[longest] + 1) % dims[longest]
    return entries.at[tuple(spot)].set(top_value)


def steps_of(key, dims, shards, smallest, high):
    level, own = 1.0, jax.random.fold_in(key, 6)
    for position, parts in shards:
        heights = jnp.exp(jax.random.uniform(jax.random.fold_in(own, position), (parts,), jnp.float32, smallest / len(shards), high / len(shards)))
        level = level * jnp.repeat(heights, dims[position] // parts).reshape([-1 if axis == position else 1 for axis in range(len(dims))])
    return level


def gaussian(key, shape, width, most, split=(), held_as=jnp.bfloat16):
    result = width * jax.random.normal(key, shape, jnp.float32)
    if split:
        result = result * steps_of(key, shape, split, -0.22, 0.18)
    return jnp.clip(result, -most, most).astype(held_as)


def setup_inputs(seed: int = 0) -> dict:
    keys = jax.random.split(jax.random.key(seed), 9)
    rows = gaussian(keys[0], (TABLES, ROWS, E), 1.0, 6.0, ((1, 64), (2, 4)), jnp.float32)
    bag_ids = place_ends(jax.random.randint(keys[1], (SAMPLES, TABLES, BAG), 0, ROWS_DEV), jax.random.fold_in(keys[1], 1), 0, ROWS_DEV - 1).astype(jnp.int32)
    bag_lengths = draw_bag_lengths(jax.random.fold_in(keys[8], 71), 0)
    labels = place_ends((jax.random.randint(keys[3], (SAMPLES,), 0, 4) < 1).astype(jnp.int32), jax.random.fold_in(keys[3], 1), 0, 1)
    proj_weight = gaussian(keys[4], (TABLES * E, PROJ), (TABLES * E) ** -0.5, 0.09375)
    hidden_weight = gaussian(keys[5], (PROJ, HID), PROJ ** -0.5, 0.375)
    hidden_bias = gaussian(keys[6], (HID,), 0.5, 3.0, (), jnp.float32)
    out_weight = gaussian(keys[7], (HID,), (HID // 8) ** -0.5, 0.5, (), jnp.float32)
    return {"rows": rows, "bag_ids": bag_ids, "bag_lengths": bag_lengths, "labels": labels, "proj_weight": proj_weight, "hidden_weight": hidden_weight, "hidden_bias": hidden_bias, "out_weight": out_weight}


def bag_counts(bag_row, bag_len, row_total):
    in_bag = jnp.arange(bag_row.shape[1], dtype=jnp.int32)[None, :] < bag_len[:, None]
    matches = (bag_row[:, :, None] == jnp.arange(row_total, dtype=jnp.int32)[None, None, :]) & in_bag[:, :, None]
    return jnp.sum(matches.astype(jnp.float32), axis=1)


def contract_first(left, right):
    return lax.dot_general(left, right, (((0,), (0,)), ((), ())), preferred_element_type=jnp.float32)


def reference(rows, bag_ids, bag_lengths, labels, proj_weight, hidden_weight, hidden_bias, out_weight):
    slice_width = E // N_COL
    group_rows = rows.reshape(TABLES, N_GRP, ROWS_DEV, E).transpose(1, 0, 2, 3)
    group_ids = bag_ids.reshape(N_GRP, SAMP_GRP, TABLES, BAG)
    group_lens = bag_lengths.reshape(N_GRP, SAMP_GRP, TABLES)
    group_labels = labels.reshape(N_GRP, SAMP_GRP)

    def group_step(sums, inputs):
        rows_here, ids_here, lens_here, labels_here = inputs
        counts = [bag_counts(ids_here[:, table], lens_here[:, table], ROWS_DEV) for table in range(TABLES)]
        pooled = jnp.stack([jnp.dot(counts[table], rows_here[table], precision=lax.Precision.HIGHEST)
                            for table in range(TABLES)], axis=1).astype(jnp.bfloat16)
        features = pooled.reshape(SAMP_GRP, TABLES, N_COL, slice_width).transpose(0, 2, 1, 3)
        features = features.reshape(SAMP_GRP, N_COL * TABLES * slice_width)
        projected = jnp.dot(features, proj_weight, preferred_element_type=jnp.float32).astype(jnp.bfloat16)
        hidden_pre = jnp.dot(projected, hidden_weight, preferred_element_type=jnp.float32) + hidden_bias
        sig_pre = jax.nn.sigmoid(hidden_pre)
        active = hidden_pre * sig_pre
        logits = jnp.sum(active * out_weight, axis=1)
        slopes = jax.nn.sigmoid(logits) - labels_here.astype(jnp.float32)
        d_hidden = (slopes[:, None] * out_weight) * (sig_pre * (1.0 + hidden_pre * (1.0 - sig_pre)))
        d_hidden_b = d_hidden.astype(jnp.bfloat16)
        out_term = jnp.sum(active * slopes[:, None], axis=0)
        bias_term = jnp.sum(d_hidden, axis=0)
        hidden_term = contract_first(projected, d_hidden_b)
        d_projected = lax.dot_general(d_hidden_b, hidden_weight, (((1,), (1,)), ((), ())),
                                      preferred_element_type=jnp.float32).astype(jnp.bfloat16)
        proj_term = contract_first(features, d_projected)
        d_features = lax.dot_general(d_projected, proj_weight, (((1,), (1,)), ((), ())),
                                     preferred_element_type=jnp.float32).astype(jnp.bfloat16)
        d_pooled = d_features.reshape(SAMP_GRP, N_COL, TABLES, slice_width).transpose(0, 2, 1, 3)
        d_pooled = d_pooled.reshape(SAMP_GRP, TABLES, E).astype(jnp.float32)
        row_terms = jnp.stack([lax.dot_general(counts[table], d_pooled[:, table], (((0,), (0,)), ((), ())),
                                               precision=lax.Precision.HIGHEST)
                               for table in range(TABLES)])
        sums = (sums[0] + proj_term, sums[1] + hidden_term, sums[2] + bias_term, sums[3] + out_term)
        return sums, row_terms

    initial = (jnp.zeros((TABLES * E, PROJ), jnp.float32), jnp.zeros((PROJ, HID), jnp.float32),
               jnp.zeros((HID,), jnp.float32), jnp.zeros((HID,), jnp.float32))
    sums, row_terms = lax.scan(group_step, initial, (group_rows, group_ids, group_lens, group_labels))
    row_grad = row_terms.transpose(1, 0, 2, 3).reshape(TABLES, ROWS, E)
    return row_grad, sums[0], sums[1], sums[2], sums[3]
```

```python
import jax
import jax.numpy as jnp
from jax import lax
from jax.experimental import pallas as pl
from jax.experimental.pallas import tpu as pltpu
from jax.sharding import PartitionSpec as P

MESH = pl.DeviceIdType.MESH
BF = jnp.bfloat16
F32 = jnp.float32
NZ = 8
NP = 8
CH = 256


def mm(a, b):
    return lax.dot_general(a, b, (((1,), (0,)), ((), ())), preferred_element_type=F32)


def mm_nt(a, b):
    return lax.dot_general(a, b, (((1,), (1,)), ((), ())), preferred_element_type=F32)


def split_hi_lo(v):
    hi = v.astype(BF)
    return hi, (v - hi.astype(F32)).astype(BF)


def kernel(
    ids_ref, lens_ref, lab_ref, hw_ref, bias_ref, ow_ref, rows_hbm, pw_hbm,
    rg_hbm, proj_ref, hid_ref, bg_ref, og_ref,
    rows_ref, wc_ref, rt_ref, wct_ref, hwt_ref, bc_ref, oc_ref,
    cnt_ref, pool_ref, part_ref, ra_ref, sb_ref, rb_ref, pt_ref,
    gb_ref, act_ref, sl_ref, spt_ref, dpt_ref, dpool_ref, rg_ref,
    hs1_ref, hr1_ref, ps1_ref, pr1_ref, hs2_ref, hr2_ref, ps2_ref, pr2_ref,
    hs3_ref, hr3_ref, hr4_ref,
    in_sem, rg_sem, a_send, a_recv, b_send, b_recv, c_send, c_recv,
    h1_send, h1_recv, p1_send, p1_recv, h2_send, h2_recv, p2_send, p2_recv,
    h3_send, h3_recv, h4_send, h4_recv,
):
    c = lax.axis_index("col")
    g = lax.axis_index("grp")
    h, k = c // 2, lax.rem(c, 2)
    p, z = g // NZ, lax.rem(g, NZ)
    tables, _, samples = ids_ref.shape
    bag = ids_ref.shape[1]
    row_total = rows_ref.shape[1]
    width = rows_ref.shape[2]
    hid = hw_ref.shape[1]
    n_ch = samples // CH

    core_peer = {"col": 2 * h + (1 - k), "grp": g}
    chip_peer = {"col": 2 * (1 - h) + k, "grp": g}

    def plane_peer(d):
        q = lax.rem(p + d, NP)
        return q, {"col": c, "grp": q * NZ + z}

    def z_peer(d):
        q = lax.rem(z + d, NZ)
        return q, {"col": c, "grp": p * NZ + q}

    def far_peer(d):
        e = lax.rem(h * NP + p + d, 2 * NP)
        qh, qp = e // NP, lax.rem(e, NP)
        return e, {"col": 2 * qh + k, "grp": qp * NZ + z}

    def rows_copy(t):
        return pltpu.make_async_copy(rows_hbm.at[t], rows_ref.at[t], in_sem.at[t])

    w_copy = pltpu.make_async_copy(
        pw_hbm.at[pl.ds(pl.multiple_of(c * tables * width, 256), tables * width)], wc_ref, in_sem.at[tables]
    )
    for t in range(tables):
        rows_copy(t).start()
    w_copy.start()

    barrier = pltpu.get_barrier_semaphore()
    pl.semaphore_signal(barrier, inc=1, device_id=core_peer, device_id_type=MESH)

    def greet_far(d, carry):
        pl.semaphore_signal(barrier, inc=1, device_id=far_peer(d)[1], device_id_type=MESH)
        return carry

    def greet_z(d, carry):
        pl.semaphore_signal(barrier, inc=1, device_id=z_peer(d)[1], device_id_type=MESH)
        return carry

    lax.fori_loop(1, 2 * NP, greet_far, 0)
    lax.fori_loop(1, NZ, greet_z, 0)

    hwt_ref[...] = hw_ref[...].T
    bc_ref[...] = jnp.broadcast_to(bias_ref[...], (128, hid)).T
    oc_ref[...] = jnp.broadcast_to(ow_ref[...], (128, hid)).T
    for t in range(tables):
        rows_copy(t).wait()
        rt = rows_ref[t].T
        hi, lo = split_hi_lo(rt)
        rt_ref[t, :, :row_total] = hi
        rt_ref[t, :, row_total:] = lo
    w_copy.wait()
    wct_ref[...] = wc_ref[...].T
    pl.semaphore_wait(barrier, 2 * NP + NZ - 1)

    def cols_of(j):
        return pl.ds(pl.multiple_of(j * CH, CH), CH)

    def counts_block(j, i):
        t, b = i // 2, lax.rem(i, 2)
        cols = pl.ds(pl.multiple_of(j * CH + b * 128, 128), 128)
        ids = ids_ref[t, :, cols]
        spot = lax.broadcasted_iota(jnp.int32, (bag, 128), 0)
        ids = jnp.where(spot < lens_ref[t, :, cols], ids, -1)
        spread = [jnp.broadcast_to(ids[q : q + 1], (16, 128)).astype(jnp.int16) for q in range(bag)]
        first = lax.broadcasted_iota(jnp.int32, (16, 128), 0).astype(jnp.int16)
        one, zero = jnp.ones((16, 128), BF), jnp.zeros((16, 128), BF)
        for r in range(row_total // 16):
            row = first + jnp.int16(r * 16)
            acc = jnp.where(spread[0] == row, one, zero)
            for q in range(1, bag):
                acc = acc + jnp.where(spread[q] == row, one, zero)
            cnt_ref[t, r * 16 : (r + 1) * 16, cols] = acc

    own_half = pl.ds(pl.multiple_of(k * 128, 128), 128)
    other_half = pl.ds(pl.multiple_of((1 - k) * 128, 128), 128)

    def copy_a(j):
        return pltpu.make_async_remote_copy(
            part_ref.at[j, other_half], ra_ref.at[j], a_send.at[j], a_recv.at[j],
            device_id=core_peer, device_id_type=MESH)

    def copy_b(j):
        return pltpu.make_async_remote_copy(
            sb_ref.at[j], rb_ref.at[j], b_send.at[j], b_recv.at[j],
            device_id=chip_peer, device_id_type=MESH)

    def copy_c(j):
        return pltpu.make_async_remote_copy(
            pt_ref.at[j, own_half], pt_ref.at[j, own_half], c_send.at[j], c_recv.at[j],
            device_id=core_peer, device_id_type=MESH)

    def wait_c(j):
        pltpu.make_async_remote_copy(
            pt_ref.at[j, other_half], pt_ref.at[j, other_half], c_send.at[j], c_recv.at[j],
            device_id=core_peer, device_id_type=MESH).wait_recv()

    def chunk(j):
        cols = cols_of(j)

        def one_block(i, carry):
            counts_block(j, i)
            return carry

        lax.fori_loop(0, 2 * tables, one_block, 0)
        for t in range(tables):
            cnt = cnt_ref[t, :, cols]
            acc = mm(rt_ref[t, :, :row_total], cnt) + mm(rt_ref[t, :, row_total:], cnt)
            pool_ref[t * width : (t + 1) * width, cols] = acc.astype(BF)
        part_ref[j] = mm(wct_ref[...], pool_ref[:, cols])
        copy_a(j).start()

    def stage_b(j):
        copy_a(j).wait_recv()
        sb_ref[j] = (part_ref[j, own_half] + ra_ref[j]).astype(BF)
        copy_b(j).start()

    def stage_c(j):
        copy_b(j).wait_recv()
        pt_ref[j, own_half] = (sb_ref[j].astype(F32) + rb_ref[j].astype(F32)).astype(BF)
        copy_c(j).start()

    def mlp(j):
        wait_c(j)
        cols = cols_of(j)
        pt = pt_ref[j]
        logits = jnp.zeros((1, CH), F32)
        for q in range(hid // 256):
            hs = slice(q * 256, (q + 1) * 256)
            bias = jnp.concatenate([bc_ref[hs, :]] * (CH // 128), axis=1)
            ow = jnp.concatenate([oc_ref[hs, :]] * (CH // 128), axis=1)
            pre = mm(hwt_ref[hs, :], pt) + bias
            sig = 0.5 * jnp.tanh(0.5 * pre) + 0.5
            act = pre * sig
            logits = logits + jnp.sum(act * ow, axis=0, keepdims=True)
            gb_ref[hs, cols] = (ow * (sig + act * (1.0 - sig))).astype(BF)
            act_ref[hs, cols] = act.astype(BF)
        slopes = 0.5 * jnp.tanh(0.5 * logits) + 0.5 - lab_ref[:, cols].astype(F32)
        hi, lo = split_hi_lo(slopes)
        spot = lax.broadcasted_iota(jnp.int32, (16, CH), 0)
        sl_ref[:, cols] = jnp.where(
            spot == 0, hi.astype(F32), jnp.where(spot == 1, lo.astype(F32), 0.0)
        ).astype(BF)
        dpt_ref[:, cols] = (mm(hw_ref[...], gb_ref[:, cols]) * slopes).astype(BF)
        spt_ref[:, cols] = (pt.astype(F32) * slopes).astype(BF)

    for j in range(n_ch):
        chunk(j)
        if j >= 1:
            stage_b(j - 1)
        if j >= 2:
            stage_c(j - 2)
    stage_b(n_ch - 1)
    mlp(0)
    stage_c(n_ch - 2)
    mlp(1)
    stage_c(n_ch - 1)
    mlp(2)
    mlp(3)

    hs = pl.ds(pl.multiple_of(c * 256, 256), 256)
    g_own = gb_ref[hs, :]
    hgrad = mm_nt(spt_ref[...], g_own)
    brow = mm_nt(sl_ref[...], g_own)
    orow = mm_nt(sl_ref[...], act_ref[hs, :])

    def vec_rows(bias_row, out_row):
        bh, bl = split_hi_lo(bias_row)
        oh, ol = split_hi_lo(out_row)
        spot = lax.broadcasted_iota(jnp.int32, (16, 256), 0)
        out = jnp.zeros((16, 256), F32)
        for place, v in enumerate((bh, bl, oh, ol)):
            out = jnp.where(spot == place, v.astype(F32), out)
        return out.astype(BF)

    vec = vec_rows(brow[0:1] + brow[1:2], orow[0:1] + orow[1:2])
    for q in range(NP):
        hs1_ref[q, :32] = hgrad[q * 32 : (q + 1) * 32].astype(BF)
        hs1_ref[q, 32:] = vec

    def h1_copy(q, dev):
        return pltpu.make_async_remote_copy(
            hs1_ref.at[q], hr1_ref.at[p], h1_send.at[q], h1_recv.at[p], device_id=dev, device_id_type=MESH)

    def p1_copy(q, dev):
        return pltpu.make_async_remote_copy(
            ps1_ref.at[q], pr1_ref.at[p], p1_send.at[q], p1_recv.at[p], device_id=dev, device_id_type=MESH)

    def h2_copy(q, dev):
        return pltpu.make_async_remote_copy(
            hs2_ref, hr2_ref.at[z], h2_send.at[q], h2_recv.at[z], device_id=dev, device_id_type=MESH)

    def p2_copy(q, dev):
        return pltpu.make_async_remote_copy(
            ps2_ref.at[q], pr2_ref.at[z], p2_send.at[q], p2_recv.at[z], device_id=dev, device_id_type=MESH)

    def h3_copy(e, dev):
        own = h * NP + p
        return pltpu.make_async_remote_copy(
            hs3_ref, hr3_ref.at[own], h3_send.at[e], h3_recv.at[own], device_id=dev, device_id_type=MESH)

    def start_all(peer, copy, count):
        def go(d, carry):
            copy(*peer(d)).start()
            return carry

        lax.fori_loop(1, count, go, 0)

    def wait_all(peer, src, dst_slots, send, recv, count):
        def go(d, carry):
            q, dev = peer(d)
            pltpu.make_async_remote_copy(
                src(q), dst_slots.at[q], send.at[q], recv.at[q], device_id=dev, device_id_type=MESH).wait_recv()
            return carry

        lax.fori_loop(1, count, go, 0)

    def wait_sent(peer, copy, count):
        def go(d, carry):
            copy(*peer(d)).wait_send()
            return carry

        lax.fori_loop(1, count, go, 0)

    start_all(plane_peer, h1_copy, NP)
    hr1_ref[p] = hs1_ref[p]

    for t in range(tables):
        pg = mm_nt(pool_ref[t * width : (t + 1) * width], dpt_ref[...])
        half = NP // tables
        for q in range(half):
            ps1_ref[t * half + q] = pg[q * 128 : (q + 1) * 128].astype(BF)
    start_all(plane_peer, p1_copy, NP)
    pr1_ref[p] = ps1_ref[p]

    def row_grad(t):
        ws = slice(t * width, (t + 1) * width)
        dpool_ref[ws] = mm(wc_ref[ws], dpt_ref[...]).astype(BF)
        rg_ref[t] = mm_nt(cnt_ref[t], dpool_ref[ws])
        pltpu.make_async_copy(rg_ref.at[t], rg_hbm.at[t], rg_sem.at[t]).start()

    def slot_sum(ref, rows):
        acc = ref[0, rows].astype(F32)
        for q in range(1, NP):
            acc = acc + ref[q, rows].astype(F32)
        return acc

    row_grad(0)

    wait_all(plane_peer, lambda q: hs1_ref.at[q], hr1_ref, h1_send, h1_recv, NP)
    hs2_ref[:32] = slot_sum(hr1_ref, slice(0, 32)).astype(BF)
    v = slot_sum(hr1_ref, slice(32, 48))
    hs2_ref[32:] = vec_rows(v[0:1] + v[1:2], v[2:3] + v[3:4])
    start_all(z_peer, h2_copy, NZ)
    hr2_ref[z] = hs2_ref[...]

    row_grad(1)

    wait_all(plane_peer, lambda q: ps1_ref.at[q], pr1_ref, p1_send, p1_recv, NP)
    for q in range(NZ):
        ps2_ref[q] = slot_sum(pr1_ref, slice(q * 16, (q + 1) * 16)).astype(BF)
    start_all(z_peer, p2_copy, NZ)
    pr2_ref[z] = ps2_ref[z]

    wait_all(z_peer, lambda q: hs2_ref, hr2_ref, h2_send, h2_recv, NZ)
    hs3_ref[:32] = slot_sum(hr2_ref, slice(0, 32)).astype(BF)
    v = slot_sum(hr2_ref, slice(32, 48))
    hs3_ref[32:] = vec_rows(v[0:1] + v[1:2], v[2:3] + v[3:4])
    start_all(far_peer, h3_copy, 2 * NP)
    hr3_ref[h * NP + p] = hs3_ref[...]

    row_grad(2)
    row_grad(3)

    wait_all(z_peer, lambda q: ps2_ref.at[q], pr2_ref, p2_send, p2_recv, NZ)
    proj_ref[...] = slot_sum(pr2_ref, slice(0, 16))

    wait_all(far_peer, lambda e: hs3_ref, hr3_ref, h3_send, h3_recv, 2 * NP)
    h4 = pltpu.make_async_remote_copy(
        hr3_ref, hr4_ref, h4_send, h4_recv, device_id=core_peer, device_id_type=MESH)
    h4.start()

    def put(ref, core):
        for qh in range(2):
            col = pl.ds(pl.multiple_of((2 * qh + core) * 256, 256), 256)
            for q in range(NP):
                hid_ref[q * 32 : (q + 1) * 32, col] = ref[qh * NP + q, :32].astype(F32)
            v = ref[qh * NP, 32:].astype(F32)
            bg_ref[:, col] = v[0:1] + v[1:2]
            og_ref[:, col] = v[2:3] + v[3:4]

    put(hr3_ref, k)
    h4.wait()
    put(hr4_ref, 1 - k)

    for j in range(n_ch):
        copy_a(j).wait_send()
        copy_b(j).wait_send()
        copy_c(j).wait_send()
    wait_sent(plane_peer, h1_copy, NP)
    wait_sent(plane_peer, p1_copy, NP)
    wait_sent(z_peer, h2_copy, NZ)
    wait_sent(z_peer, p2_copy, NZ)
    wait_sent(far_peer, h3_copy, 2 * NP)
    for t in range(tables):
        pltpu.make_async_copy(rg_ref.at[t], rg_hbm.at[t], rg_sem.at[t]).wait()


def body(rows, bag_ids, bag_lengths, labels, proj_weight, hidden_weight, hidden_bias, out_weight):
    tables, row_total, width = rows.shape
    samples, _, bag = bag_ids.shape
    feats, proj = proj_weight.shape
    hid = hidden_weight.shape[1]
    own = tables * width
    n_ch = samples // CH
    ids = bag_ids.transpose(1, 2, 0)
    lens = bag_lengths.T.reshape(tables, 1, samples)
    vm = pl.BlockSpec(memory_space=pltpu.VMEM)
    hbm = pl.BlockSpec(memory_space=pl.ANY)
    dma = pltpu.SemaphoreType.DMA
    out = pl.pallas_call(
        kernel,
        out_shape=(
            jax.ShapeDtypeStruct(rows.shape, F32),
            jax.ShapeDtypeStruct((feats // 256, proj), F32),
            jax.ShapeDtypeStruct((proj, hid), F32),
            jax.ShapeDtypeStruct((1, hid), F32),
            jax.ShapeDtypeStruct((1, hid), F32),
        ),
        in_specs=[vm] * 6 + [hbm] * 2,
        out_specs=(hbm, vm, vm, vm, vm),
        scratch_shapes=[
            pltpu.VMEM((tables, row_total, width), F32),
            pltpu.VMEM((own, proj), BF),
            pltpu.VMEM((tables, width, 2 * row_total), BF),
            pltpu.VMEM((proj, own), BF),
            pltpu.VMEM((hid, proj), BF),
            pltpu.VMEM((hid, 128), F32),
            pltpu.VMEM((hid, 128), F32),
            pltpu.VMEM((tables, row_total, samples), BF),
            pltpu.VMEM((own, samples), BF),
            pltpu.VMEM((n_ch, proj, CH), F32),
            pltpu.VMEM((n_ch, proj // 2, CH), F32),
            pltpu.VMEM((n_ch, proj // 2, CH), BF),
            pltpu.VMEM((n_ch, proj // 2, CH), BF),
            pltpu.VMEM((n_ch, proj, CH), BF),
            pltpu.VMEM((hid, samples), BF),
            pltpu.VMEM((hid, samples), BF),
            pltpu.VMEM((16, samples), BF),
            pltpu.VMEM((proj, samples), BF),
            pltpu.VMEM((proj, samples), BF),
            pltpu.VMEM((own, samples), BF),
            pltpu.VMEM((tables, row_total, width), F32),
            pltpu.VMEM((NP, 48, 256), BF),
            pltpu.VMEM((NP, 48, 256), BF),
            pltpu.VMEM((NP, 128, proj), BF),
            pltpu.VMEM((NP, 128, proj), BF),
            pltpu.VMEM((48, 256), BF),
            pltpu.VMEM((NZ, 48, 256), BF),
            pltpu.VMEM((NZ, 16, proj), BF),
            pltpu.VMEM((NZ, 16, proj), BF),
            pltpu.VMEM((48, 256), BF),
            pltpu.VMEM((2 * NP, 48, 256), BF),
            pltpu.VMEM((2 * NP, 48, 256), BF),
            dma((tables + 1,)),
            dma((tables,)),
            dma((n_ch,)), dma((n_ch,)), dma((n_ch,)), dma((n_ch,)), dma((n_ch,)), dma((n_ch,)),
            dma((NP,)), dma((NP,)), dma((NP,)), dma((NP,)),
            dma((NZ,)), dma((NZ,)), dma((NZ,)), dma((NZ,)),
            dma((2 * NP,)), dma((2 * NP,)),
            dma(()), dma(()),
        ],
        compiler_params=pltpu.CompilerParams(
            collective_id=0, has_side_effects=True, vmem_limit_bytes=52 * 1024 * 1024
        ),
    )(
        ids, lens, labels.reshape(1, samples), hidden_weight, hidden_bias.reshape(1, hid),
        out_weight.reshape(1, hid), rows, proj_weight,
    )
    return out[0], out[1], out[2], out[3].reshape(hid), out[4].reshape(hid)


def solution(mesh):
    return jax.shard_map(
        body,
        mesh=mesh,
        in_specs=(
            P(None, "grp", "col"),
            P("grp", None, None),
            P("grp", None),
            P("grp"),
            P(),
            P(),
            P(),
            P(),
        ),
        out_specs=(P(None, "grp", "col"), P(("col", "grp"), None), P(), P(), P()),
        check_vma=False,
    )
```

```python
import jax
import jax.numpy as jnp
from jax import lax
from jax.experimental import pallas as pl
from jax.experimental.pallas import tpu as pltpu
from jax.sharding import PartitionSpec as P

MESH = pl.DeviceIdType.MESH
BF = jnp.bfloat16
F32 = jnp.float32
NZ = 8
NP = 8
CH = 256


def mm(a, b):
    return lax.dot_general(a, b, (((1,), (0,)), ((), ())), preferred_element_type=F32)


def mm_nt(a, b):
    return lax.dot_general(a, b, (((1,), (1,)), ((), ())), preferred_element_type=F32)


def split_hi_lo(v):
    hi = v.astype(BF)
    return hi, (v - hi.astype(F32)).astype(BF)


def kernel(
    ids_hbm, lens_hbm, lab_hbm, hw_hbm, bias_hbm, ow_hbm, rows_hbm, pw_hbm,
    rg_hbm, proj_hbm, hr_hbm, vec_hbm,
    rg_ref, proj_ref, ids_ref, lens_ref, lab_ref, hw_ref, bias_ref, ow_ref, mid_ref, rows_ref,
    wc_ref, rt_ref, wct_ref, hwt_ref, bc_ref, oc_ref,
    cnt_ref, pool_ref, part_ref, ra_ref, sb_ref, rb_ref, pt_ref,
    gb_ref, act_ref, sl_ref, spt_ref, dpt_ref, dpool_ref,
    hs1_ref, hr1_ref, ps1_ref, pr1_ref, hs2_ref, hr2_ref, ps2_ref, pr2_ref,
    hs3_ref, hr3_ref, vs1_ref, vr1_ref, vs2_ref, vr2_ref, vs3_ref, vr3_ref,
    in_sem, out_sem, n_send, n_recv, a_send, a_recv, b_send, b_recv, c_send, c_recv,
    h1_send, h1_recv, p1_send, p1_recv, h2_send, h2_recv, p2_send, p2_recv,
    h3_send, h3_recv, h4_send, h4_recv,
    v1_send, v1_recv, v2_send, v2_recv, v3_send, v3_recv, v4_send, v4_recv,
):
    c = lax.axis_index("col")
    g = lax.axis_index("grp")
    h, k = c // 2, lax.rem(c, 2)
    p, z = g // NZ, lax.rem(g, NZ)
    tables, _, samples = ids_ref.shape
    bag = ids_ref.shape[1]
    row_total = rows_ref.shape[1]
    width = rows_ref.shape[2]
    hid = hw_ref.shape[1]
    n_ch = samples // CH

    core_peer = {"col": 2 * h + (1 - k), "grp": g}
    chip_peer = {"col": 2 * (1 - h) + k, "grp": g}

    def plane_peer(d):
        q = lax.rem(p + d, NP)
        return q, {"col": c, "grp": q * NZ + z}

    def z_peer(d):
        q = lax.rem(z + d, NZ)
        return q, {"col": c, "grp": p * NZ + q}

    def far_peer(d):
        e = lax.rem(h * NP + p + d, 2 * NP)
        qh, qp = e // NP, lax.rem(e, NP)
        return e, {"col": 2 * qh + k, "grp": qp * NZ + z}

    def rows_copy(t):
        return pltpu.make_async_copy(rows_hbm.at[t], rows_ref.at[t], in_sem.at[t])

    own_w = pw_hbm.at[pl.ds(pl.multiple_of(c * tables * width, 256), tables * width)]
    small = [
        pltpu.make_async_copy(src, dst, in_sem.at[tables + n])
        for n, (src, dst) in enumerate((
            (ids_hbm, ids_ref), (lens_hbm, lens_ref), (hw_hbm, hw_ref), (bias_hbm, bias_ref),
            (ow_hbm, ow_ref), (lab_hbm, lab_ref), (own_w, wc_ref)))
    ]
    for copy in small[:2]:
        copy.start()
    for t in range(tables):
        rows_copy(t).start()
    for copy in small[2:]:
        copy.start()

    barrier = pltpu.get_barrier_semaphore()
    pl.semaphore_signal(barrier, inc=1, device_id=core_peer, device_id_type=MESH)

    def greet_far(d, carry):
        pl.semaphore_signal(barrier, inc=1, device_id=far_peer(d)[1], device_id_type=MESH)
        return carry

    def greet_z(d, carry):
        pl.semaphore_signal(barrier, inc=1, device_id=z_peer(d)[1], device_id_type=MESH)
        return carry

    lax.fori_loop(1, 2 * NP, greet_far, 0)
    lax.fori_loop(1, NZ, greet_z, 0)

    def cols_of(j):
        return pl.ds(pl.multiple_of(j * CH, CH), CH)

    n_own = tables // 2

    def copy_n(j, i):
        t = k * n_own + i
        return pltpu.make_async_remote_copy(
            cnt_ref.at[j, t], cnt_ref.at[j, t], n_send.at[j * n_own + i], n_recv.at[j * n_own + i],
            device_id=core_peer, device_id_type=MESH)

    def wait_n(j, i):
        t = (1 - k) * n_own + i
        pltpu.make_async_remote_copy(
            cnt_ref.at[j, t], cnt_ref.at[j, t], n_send.at[j * n_own + i], n_recv.at[j * n_own + i],
            device_id=core_peer, device_id_type=MESH).wait_recv()

    def counts(j, send):
        lanes = CH // 128

        def block(n, carry):
            i, b = n // lanes, lax.rem(n, lanes)
            t = k * n_own + i
            ids = mid_ref[t, :, pl.ds(pl.multiple_of(j * CH + b * 128, 128), 128)]
            cols = pl.ds(pl.multiple_of(b * 128, 128), 128)
            spread = [jnp.broadcast_to(ids[q : q + 1], (16, 128)).astype(jnp.int16) for q in range(bag)]
            first = lax.broadcasted_iota(jnp.int32, (16, 128), 0).astype(jnp.int16)
            one, zero = jnp.ones((16, 128), BF), jnp.zeros((16, 128), BF)
            for r in range(row_total // 16):
                row = first + jnp.int16(r * 16)
                acc = jnp.where(spread[0] == row, one, zero)
                for q in range(1, bag):
                    acc = acc + jnp.where(spread[q] == row, one, zero)
                cnt_ref[j, t, r * 16 : (r + 1) * 16, cols] = acc
            if send:
                @pl.when(b == lanes - 1)
                def _():
                    copy_n(j, i).start()

            return carry

        lax.fori_loop(0, n_own * lanes, block, 0)

    def pool_block(j, t):
        ws = pl.ds(pl.multiple_of(t * width, width), width)
        both = mm(rt_ref[t], cnt_ref[j, t])
        pool_ref[ws, cols_of(j)] = (both[:width] + both[width:]).astype(BF)

    def pool_own(j):
        for i in range(n_own):
            pool_block(j, k * n_own + i)

    def pool_other(j):
        for i in range(n_own):
            wait_n(j, i)
            pool_block(j, (1 - k) * n_own + i)
        part_ref[j] = mm(wct_ref[...], pool_ref[:, cols_of(j)])
        copy_a(j).start()

    own_half = pl.ds(pl.multiple_of(k * 128, 128), 128)
    other_half = pl.ds(pl.multiple_of((1 - k) * 128, 128), 128)

    def copy_a(j):
        return pltpu.make_async_remote_copy(
            part_ref.at[j, other_half], ra_ref.at[j], a_send.at[j], a_recv.at[j],
            device_id=core_peer, device_id_type=MESH)

    def copy_b(j):
        return pltpu.make_async_remote_copy(
            sb_ref.at[j], rb_ref.at[j], b_send.at[j], b_recv.at[j],
            device_id=chip_peer, device_id_type=MESH)

    def copy_c(j):
        return pltpu.make_async_remote_copy(
            pt_ref.at[j, own_half], pt_ref.at[j, own_half], c_send.at[j], c_recv.at[j],
            device_id=core_peer, device_id_type=MESH)

    def wait_c(j):
        pltpu.make_async_remote_copy(
            pt_ref.at[j, other_half], pt_ref.at[j, other_half], c_send.at[j], c_recv.at[j],
            device_id=core_peer, device_id_type=MESH).wait_recv()

    def stage_b(j):
        copy_a(j).wait_recv()
        sb_ref[j] = (part_ref[j, own_half] + ra_ref[j]).astype(BF)
        copy_b(j).start()

    def stage_c(j):
        copy_b(j).wait_recv()
        pt_ref[j, own_half] = (sb_ref[j].astype(F32) + rb_ref[j].astype(F32)).astype(BF)
        copy_c(j).start()

    def mlp(j):
        wait_c(j)
        cols = cols_of(j)
        pt = pt_ref[j]
        logits = jnp.zeros((1, CH), F32)
        for q in range(hid // 256):
            hs = pl.ds(pl.multiple_of(lax.rem(c + q, hid // 256) * 256, 256), 256)
            bias = jnp.concatenate([bc_ref[hs, :]] * (CH // 128), axis=1)
            ow = jnp.concatenate([oc_ref[hs, :]] * (CH // 128), axis=1)
            pre = mm(hwt_ref[hs, :], pt) + bias
            sig = 0.5 * jnp.tanh(0.5 * pre) + 0.5
            act = pre * sig
            logits = logits + jnp.sum(act * ow, axis=0, keepdims=True)
            gb_ref[hs, cols] = (ow * (sig + act * (1.0 - sig))).astype(BF)
            if q == 0:
                act_ref[:, cols] = act.astype(BF)
        slopes = 0.5 * jnp.tanh(0.5 * logits) + 0.5 - lab_ref[:, cols].astype(F32)
        hi, lo = split_hi_lo(slopes)
        spot = lax.broadcasted_iota(jnp.int32, (16, CH), 0)
        sl_ref[:, cols] = jnp.where(
            spot == 0, hi.astype(F32), jnp.where(spot == 1, lo.astype(F32), 0.0)
        ).astype(BF)
        dpt_ref[:, cols] = (mm(hw_ref[...], gb_ref[:, cols]) * slopes).astype(BF)
        spt_ref[:, cols] = (pt.astype(F32) * slopes).astype(BF)

    small[0].wait()
    small[1].wait()
    for t in range(tables):
        spot = lax.broadcasted_iota(jnp.int32, (bag, samples), 0)
        mid_ref[t] = jnp.where(spot < lens_ref[t : t + 1, :], ids_ref[t], -1)
    counts(0, False)
    for t in range(tables):
        rows_copy(t).wait()
        hi, lo = split_hi_lo(rows_ref[t].T)
        rt_ref[t, :width] = hi
        rt_ref[t, width:] = lo
    small[6].wait()
    wct_ref[...] = wc_ref[...].T
    pl.semaphore_wait(barrier, 2 * NP + NZ - 1)
    for i in range(n_own):
        copy_n(0, i).start()
    pool_own(0)
    for j in range(1, n_ch):
        counts(j, True)
        if j >= 2:
            stage_b(j - 2)
        pool_other(j - 1)
        pool_own(j)
    stage_c(0)
    stage_b(n_ch - 2)
    pool_other(n_ch - 1)
    for copy in small[2:6]:
        copy.wait()
    hwt_ref[...] = hw_ref[...].T
    bc_ref[...] = jnp.broadcast_to(bias_ref[...], (128, hid)).T
    oc_ref[...] = jnp.broadcast_to(ow_ref[...], (128, hid)).T
    stage_b(n_ch - 1)
    mlp(0)
    for j in range(1, n_ch):
        stage_c(j)
        mlp(j)

    hs = pl.ds(pl.multiple_of(c * 256, 256), 256)
    g_own = gb_ref[hs, :]
    hgrad = mm_nt(spt_ref[...], g_own)
    brow = mm_nt(sl_ref[...], g_own)
    orow = mm_nt(sl_ref[...], act_ref[...])

    hs1_ref[...] = hgrad.astype(BF).reshape(NP, 32, 256)
    spot = lax.broadcasted_iota(jnp.int32, (8, 256), 0)
    vs1_ref[...] = jnp.where(
        spot == 0, brow[0:1] + brow[1:2], jnp.where(spot == 1, orow[0:1] + orow[1:2], 0.0))

    def h1_copy(q, dev):
        return pltpu.make_async_remote_copy(
            hs1_ref.at[q], hr1_ref.at[p], h1_send.at[q], h1_recv.at[p], device_id=dev, device_id_type=MESH)

    def p1_copy(q, dev):
        return pltpu.make_async_remote_copy(
            ps1_ref.at[q], pr1_ref.at[p], p1_send.at[q], p1_recv.at[p], device_id=dev, device_id_type=MESH)

    def h2_copy(q, dev):
        return pltpu.make_async_remote_copy(
            hs2_ref, hr2_ref.at[z], h2_send.at[q], h2_recv.at[z], device_id=dev, device_id_type=MESH)

    def p2_copy(q, dev):
        return pltpu.make_async_remote_copy(
            ps2_ref.at[q], pr2_ref.at[z], p2_send.at[q], p2_recv.at[z], device_id=dev, device_id_type=MESH)

    def h3_copy(e, dev):
        own = h * NP + p
        return pltpu.make_async_remote_copy(
            hs3_ref, hr3_ref.at[own], h3_send.at[e], h3_recv.at[own], device_id=dev, device_id_type=MESH)

    def v1_copy(dev):
        return pltpu.make_async_remote_copy(
            vs1_ref, vr1_ref.at[p], v1_send, v1_recv.at[p], device_id=dev, device_id_type=MESH)

    def v2_copy(q, dev):
        return pltpu.make_async_remote_copy(
            vs2_ref, vr2_ref.at[z], v2_send.at[q], v2_recv.at[z], device_id=dev, device_id_type=MESH)

    def v3_copy(e, dev):
        return pltpu.make_async_remote_copy(
            vs3_ref, vr3_ref.at[h], v3_send.at[e], v3_recv.at[h], device_id=dev, device_id_type=MESH)

    def v3_from(qh):
        return pltpu.make_async_remote_copy(
            vs3_ref, vr3_ref.at[qh], v3_send.at[0], v3_recv.at[qh],
            device_id={"col": 2 * qh + k, "grp": (2 * qh + k) * NZ + z}, device_id_type=MESH)

    vec_peer = {"col": c, "grp": c * NZ + z}

    def start_all(peer, copy, count):
        def go(d, carry):
            copy(*peer(d)).start()
            return carry

        lax.fori_loop(1, count, go, 0)

    def wait_all(peer, src, dst_slots, send, recv, count):
        def go(d, carry):
            q, dev = peer(d)
            pltpu.make_async_remote_copy(
                src(q), dst_slots.at[q], send.at[q], recv.at[q], device_id=dev, device_id_type=MESH).wait_recv()
            return carry

        lax.fori_loop(1, count, go, 0)

    def wait_sent(peer, copy, count):
        def go(d, carry):
            copy(*peer(d)).wait_send()
            return carry

        lax.fori_loop(1, count, go, 0)

    start_all(plane_peer, h1_copy, NP)

    @pl.when(p != c)
    def _():
        v1_copy(vec_peer).start()

    @pl.when(p == c)
    def _():
        vr1_ref[p] = vs1_ref[...]

    hr1_ref[p] = hs1_ref[p]

    for t in range(tables):
        pg = mm_nt(pool_ref[t * width : (t + 1) * width], dpt_ref[...])
        half = NP // tables
        for q in range(half):
            ps1_ref[t * half + q] = pg[q * 128 : (q + 1) * 128].astype(BF)
    start_all(plane_peer, p1_copy, NP)
    pr1_ref[p] = ps1_ref[p]

    def row_grad(t):
        ws = slice(t * width, (t + 1) * width)
        dpool_ref[ws] = mm(wc_ref[ws], dpt_ref[...]).astype(BF)
        acc = mm_nt(cnt_ref[0, t], dpool_ref[ws, :CH])
        for j in range(1, n_ch):
            acc = acc + mm_nt(cnt_ref[j, t], dpool_ref[ws, j * CH : (j + 1) * CH])
        rg_ref[t] = acc
        pltpu.make_async_copy(rg_ref.at[t], rg_hbm.at[t], out_sem.at[t]).start()

    def slot_sum(ref, rows):
        acc = ref[0, rows].astype(F32)
        for q in range(1, NP):
            acc = acc + ref[q, rows].astype(F32)
        return acc

    row_grad(0)

    wait_all(plane_peer, lambda q: hs1_ref.at[q], hr1_ref, h1_send, h1_recv, NP)
    hs2_ref[...] = slot_sum(hr1_ref, slice(0, 32)).astype(BF)
    start_all(z_peer, h2_copy, NZ)
    hr2_ref[z] = hs2_ref[...]

    @pl.when(p == c)
    def _():
        wait_all(plane_peer, lambda q: vs1_ref, vr1_ref, v2_send, v1_recv, NP)
        vs2_ref[...] = slot_sum(vr1_ref, slice(0, 8))
        start_all(z_peer, v2_copy, NZ)
        vr2_ref[z] = vs2_ref[...]

    row_grad(1)

    wait_all(plane_peer, lambda q: ps1_ref.at[q], pr1_ref, p1_send, p1_recv, NP)
    for q in range(NZ):
        ps2_ref[q] = slot_sum(pr1_ref, slice(q * 16, (q + 1) * 16)).astype(BF)
    start_all(z_peer, p2_copy, NZ)
    pr2_ref[z] = ps2_ref[z]

    wait_all(z_peer, lambda q: hs2_ref, hr2_ref, h2_send, h2_recv, NZ)
    hs3_ref[...] = slot_sum(hr2_ref, slice(0, 32)).astype(BF)
    start_all(far_peer, h3_copy, 2 * NP)
    hr3_ref[h * NP + p] = hs3_ref[...]

    @pl.when(p == c)
    def _():
        wait_all(z_peer, lambda q: vs2_ref, vr2_ref, v2_send, v2_recv, NZ)
        vs3_ref[...] = slot_sum(vr2_ref, slice(0, 8))
        start_all(far_peer, v3_copy, 2 * NP)
        vr3_ref[h] = vs3_ref[...]

    row_grad(2)
    row_grad(3)

    wait_all(z_peer, lambda q: ps2_ref.at[q], pr2_ref, p2_send, p2_recv, NZ)
    proj_ref[...] = slot_sum(pr2_ref, slice(0, 16))
    proj_out = pltpu.make_async_copy(proj_ref, proj_hbm, out_sem.at[tables])
    proj_out.start()

    wait_all(far_peer, lambda e: hs3_ref, hr3_ref, h3_send, h3_recv, 2 * NP)
    h4 = pltpu.make_async_remote_copy(
        hr3_ref, hr_hbm.at[k], h4_send, h4_recv, device_id=core_peer, device_id_type=MESH)
    h4.start()
    hr_out = pltpu.make_async_copy(hr3_ref, hr_hbm.at[k], out_sem.at[tables + 1])
    hr_out.start()
    for qh in range(2):
        @pl.when((h != qh) | (p != c))
        def _():
            v3_from(qh).wait_recv()

    v4 = pltpu.make_async_remote_copy(
        vr3_ref, vec_hbm.at[k], v4_send, v4_recv, device_id=core_peer, device_id_type=MESH)
    v4.start()
    vec_out = pltpu.make_async_copy(vr3_ref, vec_hbm.at[k], out_sem.at[tables + 2])
    vec_out.start()

    for j in range(n_ch):
        copy_a(j).wait_send()
        copy_b(j).wait_send()
        copy_c(j).wait_send()
        for i in range(n_own):
            copy_n(j, i).wait_send()
    wait_sent(plane_peer, h1_copy, NP)
    wait_sent(plane_peer, p1_copy, NP)
    wait_sent(z_peer, h2_copy, NZ)
    wait_sent(z_peer, p2_copy, NZ)
    wait_sent(far_peer, h3_copy, 2 * NP)
    for t in range(tables):
        pltpu.make_async_copy(rg_ref.at[t], rg_hbm.at[t], out_sem.at[t]).wait()
    @pl.when(p != c)
    def _():
        v1_copy(vec_peer).wait_send()

    @pl.when(p == c)
    def _():
        wait_sent(z_peer, v2_copy, NZ)
        wait_sent(far_peer, v3_copy, 2 * NP)

    proj_out.wait()
    hr_out.wait()
    vec_out.wait()
    h4.wait_send()
    v4.wait_send()
    pltpu.make_async_remote_copy(
        hr3_ref, hr_hbm.at[1 - k], h4_send, h4_recv, device_id=core_peer, device_id_type=MESH).wait_recv()
    pltpu.make_async_remote_copy(
        vr3_ref, vec_hbm.at[1 - k], v4_send, v4_recv, device_id=core_peer, device_id_type=MESH).wait_recv()


def write_out(
    rg_hbm, proj_hbm, hr_hbm, vec_hbm, rg_out, proj_out, hid_out, bg_out, og_out,
    rg_ref, proj_ref, hr_ref, vec_ref, hid_ref, bg_ref, og_ref, in_sem, out_sem,
):
    tables = rg_ref.shape[0]

    def copy(src, dst, sem):
        return pltpu.make_async_copy(src, dst, sem)

    ins = [copy(hr_hbm, hr_ref, in_sem.at[0]), copy(vec_hbm, vec_ref, in_sem.at[1]), copy(proj_hbm, proj_ref, in_sem.at[2])]
    ins += [copy(rg_hbm.at[t], rg_ref.at[t], in_sem.at[3 + t]) for t in range(tables)]
    outs = [copy(rg_ref.at[t], rg_out.at[t], out_sem.at[t]) for t in range(tables)]
    outs += [
        copy(src, dst, out_sem.at[tables + n])
        for n, (src, dst) in enumerate(((proj_ref, proj_out), (hid_ref, hid_out), (bg_ref, bg_out), (og_ref, og_out)))
    ]
    for one in ins:
        one.start()
    for one in ins[:3]:
        one.wait()
    for core in range(2):
        for qh in range(2):
            col = slice((2 * qh + core) * 256, (2 * qh + core + 1) * 256)
            for q in range(NP):
                hid_ref[q * 32 : (q + 1) * 32, col] = hr_ref[core, qh * NP + q].astype(F32)
            bg_ref[:, col] = vec_ref[core, qh, 0:1]
            og_ref[:, col] = vec_ref[core, qh, 1:2]
    for one in outs[tables:]:
        one.start()
    for t in range(tables):
        ins[3 + t].wait()
        outs[t].start()
    for one in outs:
        one.wait()


def body(rows, bag_ids, bag_lengths, labels, proj_weight, hidden_weight, hidden_bias, out_weight):
    tables, row_total, width = rows.shape
    samples, _, bag = bag_ids.shape
    feats, proj = proj_weight.shape
    hid = hidden_weight.shape[1]
    own = tables * width
    n_ch = samples // CH
    ids = bag_ids.transpose(1, 2, 0)
    lens = bag_lengths.T
    hbm = pl.BlockSpec(memory_space=pl.ANY)
    dma = pltpu.SemaphoreType.DMA
    out = pl.pallas_call(
        kernel,
        out_shape=(
            jax.ShapeDtypeStruct(rows.shape, F32),
            jax.ShapeDtypeStruct((feats // 256, proj), F32),
            jax.ShapeDtypeStruct((2, 2 * NP, 32, 256), BF),
            jax.ShapeDtypeStruct((2, 2, 8, 256), F32),
        ),
        in_specs=[hbm] * 8,
        out_specs=[hbm] * 4,
        scratch_shapes=[
            pltpu.VMEM(rows.shape, F32),
            pltpu.VMEM((feats // 256, proj), F32),
            pltpu.VMEM((tables, bag, samples), jnp.int32),
            pltpu.VMEM((tables, samples), jnp.int32),
            pltpu.VMEM((1, samples), jnp.int32),
            pltpu.VMEM((proj, hid), BF),
            pltpu.VMEM((1, hid), F32),
            pltpu.VMEM((1, hid), F32),
            pltpu.VMEM((tables, bag, samples), jnp.int32),
            pltpu.VMEM((tables, row_total, width), F32),
            pltpu.VMEM((own, proj), BF),
            pltpu.VMEM((tables, 2 * width, row_total), BF),
            pltpu.VMEM((proj, own), BF),
            pltpu.VMEM((hid, proj), BF),
            pltpu.VMEM((hid, 128), F32),
            pltpu.VMEM((hid, 128), F32),
            pltpu.VMEM((n_ch, tables, row_total, CH), BF),
            pltpu.VMEM((own, samples), BF),
            pltpu.VMEM((n_ch, proj, CH), F32),
            pltpu.VMEM((n_ch, proj // 2, CH), F32),
            pltpu.VMEM((n_ch, proj // 2, CH), BF),
            pltpu.VMEM((n_ch, proj // 2, CH), BF),
            pltpu.VMEM((n_ch, proj, CH), BF),
            pltpu.VMEM((hid, samples), BF),
            pltpu.VMEM((256, samples), BF),
            pltpu.VMEM((16, samples), BF),
            pltpu.VMEM((proj, samples), BF),
            pltpu.VMEM((proj, samples), BF),
            pltpu.VMEM((own, samples), BF),
            pltpu.VMEM((NP, 32, 256), BF),
            pltpu.VMEM((NP, 32, 256), BF),
            pltpu.VMEM((NP, 128, proj), BF),
            pltpu.VMEM((NP, 128, proj), BF),
            pltpu.VMEM((32, 256), BF),
            pltpu.VMEM((NZ, 32, 256), BF),
            pltpu.VMEM((NZ, 16, proj), BF),
            pltpu.VMEM((NZ, 16, proj), BF),
            pltpu.VMEM((32, 256), BF),
            pltpu.VMEM((2 * NP, 32, 256), BF),
            pltpu.VMEM((8, 256), F32),
            pltpu.VMEM((NP, 8, 256), F32),
            pltpu.VMEM((8, 256), F32),
            pltpu.VMEM((NZ, 8, 256), F32),
            pltpu.VMEM((8, 256), F32),
            pltpu.VMEM((2, 8, 256), F32),
            dma((tables + 7,)),
            dma((tables + 3,)),
            dma((n_ch * 2,)), dma((n_ch * 2,)),
            dma((n_ch,)), dma((n_ch,)), dma((n_ch,)), dma((n_ch,)), dma((n_ch,)), dma((n_ch,)),
            dma((NP,)), dma((NP,)), dma((NP,)), dma((NP,)),
            dma((NZ,)), dma((NZ,)), dma((NZ,)), dma((NZ,)),
            dma((2 * NP,)), dma((2 * NP,)),
            dma(()), dma(()),
            dma(()), dma((NP,)), dma((NZ,)), dma((NZ,)), dma((2 * NP,)), dma((2,)), dma(()), dma(()),
        ],
        compiler_params=pltpu.CompilerParams(
            collective_id=0, has_side_effects=True, vmem_limit_bytes=64 * 1024 * 1024
        ),
    )(
        ids, lens, labels.reshape(1, samples), hidden_weight, hidden_bias.reshape(1, hid),
        out_weight.reshape(1, hid), rows, proj_weight,
    )
    shapes = (
        jax.ShapeDtypeStruct(rows.shape, F32),
        jax.ShapeDtypeStruct((feats // 256, proj), F32),
        jax.ShapeDtypeStruct((proj, hid), F32),
        jax.ShapeDtypeStruct((1, hid), F32),
        jax.ShapeDtypeStruct((1, hid), F32),
    )
    held = [pltpu.VMEM(o.shape, o.dtype) for o in (*out, *shapes[2:])]
    out = pl.pallas_call(
        write_out,
        out_shape=shapes,
        in_specs=[hbm] * 4,
        out_specs=[hbm] * 5,
        scratch_shapes=held + [dma((tables + 3,)), dma((tables + 4,))],
        compiler_params=pltpu.CompilerParams(vmem_limit_bytes=64 * 1024 * 1024),
    )(*out)
    return out[0], out[1], out[2], out[3].reshape(hid), out[4].reshape(hid)


def solution(mesh):
    return jax.shard_map(
        body,
        mesh=mesh,
        in_specs=(
            P(None, "grp", "col"),
            P("grp", None, None),
            P("grp", None),
            P("grp"),
            P(),
            P(),
            P(),
            P(),
        ),
        out_specs=(P(None, "grp", "col"), P(("col", "grp"), None), P(), P(), P()),
        check_vma=False,
    )
```

```python
import jax
import jax.numpy as jnp
from jax import lax
from jax.experimental import pallas as pl
from jax.experimental.pallas import tpu as pltpu
from jax.sharding import PartitionSpec as P

MESH = pl.DeviceIdType.MESH
BF = jnp.bfloat16
F32 = jnp.float32
NZ = 8
NP = 8
CH = 256


def mm(a, b):
    return lax.dot_general(a, b, (((1,), (0,)), ((), ())), preferred_element_type=F32)


def mm_nt(a, b):
    return lax.dot_general(a, b, (((1,), (1,)), ((), ())), preferred_element_type=F32)


def split_hi_lo(v):
    hi = v.astype(BF)
    return hi, (v - hi.astype(F32)).astype(BF)


def kernel(
    ids_hbm, lens_hbm, lab_hbm, hw_hbm, bias_hbm, ow_hbm, rows_hbm, pw_hbm,
    rg_hbm, proj_hbm, hr_hbm, vec_hbm,
    rg_ref, proj_ref, ids_ref, lens_ref, lab_ref, hw_ref, bias_ref, ow_ref, mid_ref, rows_ref,
    wc_ref, rt_ref, wct_ref, hwt_ref, bc_ref, oc_ref,
    cnt0_ref, cnt1_ref, cnt2_ref, cnt3_ref, pool_ref, part_ref, ra_ref, sb_ref, rb_ref, pt_ref,
    gb_ref, hacc_ref, oacc_ref, dpt_ref, dpool_ref,
    hs1_ref, hr1_ref, ps1_ref, pr1_ref, hs2_ref, hr2_ref, ps2_ref, pr2_ref,
    hs3_ref, hr3_ref, vs1_ref, vr1_ref, vs2_ref, vr2_ref, vs3_ref, vr3_ref,
    in_sem, out_sem, n_send, n_recv, a_send, a_recv, b_send, b_recv, c_send, c_recv,
    h1_send, h1_recv, p1_send, p1_recv, h2_send, h2_recv, p2_send, p2_recv,
    h3_send, h3_recv, h4_send, h4_recv,
    v1_send, v1_recv, v2_send, v2_recv, v3_send, v3_recv, v4_send, v4_recv,
):
    c = lax.axis_index("col")
    g = lax.axis_index("grp")
    h, k = c // 2, lax.rem(c, 2)
    p, z = g // NZ, lax.rem(g, NZ)
    tables, _, samples = ids_ref.shape
    bag = ids_ref.shape[1]
    row_total = rows_ref.shape[1]
    width = rows_ref.shape[2]
    hid = hw_ref.shape[1]
    cnts = (cnt0_ref, cnt1_ref, cnt2_ref, cnt3_ref)
    n_ch = len(cnts)

    core_peer = {"col": 2 * h + (1 - k), "grp": g}
    chip_peer = {"col": 2 * (1 - h) + k, "grp": g}

    y, x_lo = p // 2, lax.rem(p, 2)
    plane_steps = ((2, 1), (1, 1), (3, 1), (2, 0), (0, 1), (1, 0), (3, 0))
    far_steps = sorted(
        ((dy, dx) for dy in range(4) for dx in range(4) if dy or dx), key=lambda s: -min(s[0], 4 - s[0]) - min(s[1], 4 - s[1])
    )
    z_steps = (4, 3, 5, 2, 6, 1, 7)

    def plane_peer(d):
        dy, dx = plane_steps[d]
        q = lax.rem(y + dy, 4) * 2 + lax.rem(x_lo + dx, 2)
        return q, {"col": c, "grp": q * NZ + z}

    def z_peer(d):
        q = lax.rem(z + z_steps[d], NZ)
        return q, {"col": c, "grp": p * NZ + q}

    def far_peer(d):
        dy, dx = far_steps[d]
        qx = lax.rem(h * 2 + x_lo + dx, 4)
        qh, qp = qx // 2, lax.rem(y + dy, 4) * 2 + lax.rem(qx, 2)
        return qh * NP + qp, {"col": 2 * qh + k, "grp": qp * NZ + z}

    def rows_copy(t):
        return pltpu.make_async_copy(rows_hbm.at[t], rows_ref.at[t], in_sem.at[t])

    own_w = pw_hbm.at[pl.ds(pl.multiple_of(c * tables * width, 256), tables * width)]
    small = [
        pltpu.make_async_copy(src, dst, in_sem.at[tables + n])
        for n, (src, dst) in enumerate((
            (ids_hbm, ids_ref), (lens_hbm, lens_ref), (hw_hbm, hw_ref), (bias_hbm, bias_ref),
            (ow_hbm, ow_ref), (lab_hbm, lab_ref), (own_w, wc_ref)))
    ]
    for copy in small[:2]:
        copy.start()
    for t in range(tables):
        rows_copy(t).start()
    for copy in small[2:]:
        copy.start()

    barrier = pltpu.get_barrier_semaphore()
    pl.semaphore_signal(barrier, inc=1, device_id=core_peer, device_id_type=MESH)

    for d in range(2 * NP - 1):
        pl.semaphore_signal(barrier, inc=1, device_id=far_peer(d)[1], device_id_type=MESH)
    for d in range(NZ - 1):
        pl.semaphore_signal(barrier, inc=1, device_id=z_peer(d)[1], device_id_type=MESH)

    def cols_of(j):
        return pl.ds(pl.multiple_of(j * CH, CH), CH)

    n_own = tables // 2

    def copy_n(j, i):
        t = k * n_own + i
        return pltpu.make_async_remote_copy(
            cnts[j].at[t], cnts[j].at[t], n_send.at[j * n_own + i], n_recv.at[j * n_own + i],
            device_id=core_peer, device_id_type=MESH)

    def wait_n(j, i):
        t = (1 - k) * n_own + i
        pltpu.make_async_remote_copy(
            cnts[j].at[t], cnts[j].at[t], n_send.at[j * n_own + i], n_recv.at[j * n_own + i],
            device_id=core_peer, device_id_type=MESH).wait_recv()

    lanes = CH // 128

    def count_block(j, n):
        i, b = n // lanes, lax.rem(n, lanes)
        t = k * n_own + i
        ids = mid_ref[t, :, pl.ds(pl.multiple_of(j * CH + b * 128, 128), 128)]
        cols = pl.ds(pl.multiple_of(b * 128, 128), 128)
        spread = [jnp.broadcast_to(ids[q : q + 1], (16, 128)).astype(jnp.int16) for q in range(bag)]
        first = lax.broadcasted_iota(jnp.int32, (16, 128), 0).astype(jnp.int16)
        one, zero = jnp.ones((16, 128), BF), jnp.zeros((16, 128), BF)
        for r in range(row_total // 16):
            row = first + jnp.int16(r * 16)
            acc = jnp.where(spread[0] == row, one, zero)
            for q in range(1, bag):
                acc = acc + jnp.where(spread[q] == row, one, zero)
            cnts[j][t, r * 16 : (r + 1) * 16, cols] = acc

    def pool_block(j, t):
        ws = pl.ds(pl.multiple_of(t * width, width), width)
        both = mm(rt_ref[t], cnts[j][t])
        pool_ref[ws, cols_of(j)] = (both[:width] + both[width:]).astype(BF)

    def pool_own(j, i):
        pool_block(j, k * n_own + i)

    def pool_other(j, i):
        pool_block(j, (1 - k) * n_own + i)

    def counts_pool(j, own, other):
        def first(n, carry):
            pool_own(own, n)
            count_block(j, n)
            return carry

        def second(n, carry):
            if other is not None:
                pool_other(other, n - lanes)
            count_block(j, n)
            return carry

        lax.fori_loop(0, lanes, first, 0)
        if other is not None:
            copy_n(j, 0).start()
            for i in range(n_own):
                wait_n(other, i)
        lax.fori_loop(lanes, 2 * lanes, second, 0)
        if other is not None:
            copy_n(j, 1).start()

    def project(j):
        part_ref[j] = mm(wct_ref[...], pool_ref[:, cols_of(j)])
        copy_a(j).start()

    own_half = pl.ds(pl.multiple_of(k * 128, 128), 128)
    other_half = pl.ds(pl.multiple_of((1 - k) * 128, 128), 128)

    def copy_a(j):
        return pltpu.make_async_remote_copy(
            part_ref.at[j, other_half], ra_ref.at[j], a_send.at[j], a_recv.at[j],
            device_id=core_peer, device_id_type=MESH)

    def copy_b(j):
        return pltpu.make_async_remote_copy(
            sb_ref.at[j], rb_ref.at[j], b_send.at[j], b_recv.at[j],
            device_id=chip_peer, device_id_type=MESH)

    def copy_c(j):
        return pltpu.make_async_remote_copy(
            pt_ref.at[j, own_half], pt_ref.at[j, own_half], c_send.at[j], c_recv.at[j],
            device_id=core_peer, device_id_type=MESH)

    def wait_c(j):
        pltpu.make_async_remote_copy(
            pt_ref.at[j, other_half], pt_ref.at[j, other_half], c_send.at[j], c_recv.at[j],
            device_id=core_peer, device_id_type=MESH).wait_recv()

    def stage_b(j):
        copy_a(j).wait_recv()
        sb_ref[j] = (part_ref[j, own_half] + ra_ref[j]).astype(BF)
        copy_b(j).start()

    def stage_c(j):
        copy_b(j).wait_recv()
        pt_ref[j, own_half] = (sb_ref[j].astype(F32) + rb_ref[j].astype(F32)).astype(BF)
        copy_c(j).start()

    def mlp(j):
        wait_c(j)
        cols = cols_of(j)
        pt = pt_ref[j]
        logits = jnp.zeros((1, CH), F32)
        for q in range(hid // 256):
            hs = pl.ds(pl.multiple_of(lax.rem(c + q, hid // 256) * 256, 256), 256)
            bias = jnp.concatenate([bc_ref[hs, :]] * (CH // 128), axis=1)
            ow = jnp.concatenate([oc_ref[hs, :]] * (CH // 128), axis=1)
            pre = mm(hwt_ref[hs, :], pt) + bias
            sig = 0.5 * jnp.tanh(0.5 * pre) + 0.5
            act = pre * sig
            logits = logits + jnp.sum(act * ow, axis=0, keepdims=True)
            gb_ref[hs, cols] = (ow * (sig + act * (1.0 - sig))).astype(BF)
            if q == 0:
                act_own = act.astype(BF)
        slopes = 0.5 * jnp.tanh(0.5 * logits) + 0.5 - lab_ref[:, cols].astype(F32)
        hi, lo = split_hi_lo(slopes)
        spot = lax.broadcasted_iota(jnp.int32, (16, CH), 0)
        slope_rows = jnp.where(
            spot == 0, hi.astype(F32), jnp.where(spot == 1, lo.astype(F32), 0.0)
        ).astype(BF)
        dpt_ref[:, cols] = (mm(hw_ref[...], gb_ref[:, cols]) * slopes).astype(BF)
        g_own = gb_ref[pl.ds(pl.multiple_of(c * 256, 256), 256), cols]
        sp = (pt.astype(F32) * slopes).astype(BF)
        h_term = mm_nt(jnp.concatenate([sp, slope_rows], axis=0), g_own)
        o_term = mm_nt(slope_rows, act_own)
        hacc_ref[...] = h_term if j == 0 else hacc_ref[...] + h_term
        oacc_ref[...] = o_term if j == 0 else oacc_ref[...] + o_term

    small[0].wait()
    small[1].wait()
    for t in range(tables):
        spot = lax.broadcasted_iota(jnp.int32, (bag, samples), 0)
        mid_ref[t] = jnp.where(spot < lens_ref[t : t + 1, :], ids_ref[t], -1)

    def first_counts(n, carry):
        count_block(0, n)
        return carry

    lax.fori_loop(0, n_own * lanes, first_counts, 0)
    for t in range(tables):
        rows_copy(t).wait()
        hi, lo = split_hi_lo(rows_ref[t].T)
        rt_ref[t, :width] = hi
        rt_ref[t, width:] = lo
    small[6].wait()
    wct_ref[...] = wc_ref[...].T
    counts_pool(1, 0, None)
    pl.semaphore_wait(barrier, 2 * NP + NZ - 1)
    for j in range(2):
        for i in range(n_own):
            copy_n(j, i).start()
    counts_pool(2, 1, 0)
    project(0)
    counts_pool(3, 2, 1)
    project(1)
    for i in range(n_own):
        wait_n(2, i)
        pool_other(2, i)
    project(2)
    stage_b(0)
    for i in range(n_own):
        pool_own(3, i)
    stage_b(1)
    for i in range(n_own):
        wait_n(3, i)
        pool_other(3, i)
    project(3)
    stage_b(2)
    for copy in small[2:6]:
        copy.wait()
    hwt_ref[...] = hw_ref[...].T
    bc_ref[...] = jnp.broadcast_to(bias_ref[...], (128, hid)).T
    oc_ref[...] = jnp.broadcast_to(ow_ref[...], (128, hid)).T
    stage_b(3)
    stage_c(0)
    stage_c(1)
    mlp(0)
    mlp(1)
    stage_c(2)
    stage_c(3)
    mlp(2)
    mlp(3)

    hs1_ref[...] = hacc_ref[: hw_ref.shape[0]].astype(BF).reshape(NP, 32, 256)
    brow, orow = hacc_ref[hw_ref.shape[0] :], oacc_ref[...]
    spot = lax.broadcasted_iota(jnp.int32, (8, 256), 0)
    vs1_ref[...] = jnp.where(
        spot == 0, brow[0:1] + brow[1:2], jnp.where(spot == 1, orow[0:1] + orow[1:2], 0.0))

    def h1_copy(q, dev):
        return pltpu.make_async_remote_copy(
            hs1_ref.at[q], hr1_ref.at[p], h1_send.at[q], h1_recv.at[p], device_id=dev, device_id_type=MESH)

    def p1_copy(q, dev):
        return pltpu.make_async_remote_copy(
            ps1_ref.at[q], pr1_ref.at[p], p1_send.at[q], p1_recv.at[p], device_id=dev, device_id_type=MESH)

    def h2_copy(q, dev):
        return pltpu.make_async_remote_copy(
            hs2_ref, hr2_ref.at[z], h2_send.at[q], h2_recv.at[z], device_id=dev, device_id_type=MESH)

    def p2_copy(q, dev):
        return pltpu.make_async_remote_copy(
            ps2_ref.at[q], pr2_ref.at[z], p2_send.at[q], p2_recv.at[z], device_id=dev, device_id_type=MESH)

    def h3_copy(e, dev):
        own = h * NP + p
        return pltpu.make_async_remote_copy(
            hs3_ref, hr3_ref.at[own], h3_send.at[e], h3_recv.at[own], device_id=dev, device_id_type=MESH)

    def v1_copy(dev):
        return pltpu.make_async_remote_copy(
            vs1_ref, vr1_ref.at[p], v1_send, v1_recv.at[p], device_id=dev, device_id_type=MESH)

    def v2_copy(q, dev):
        return pltpu.make_async_remote_copy(
            vs2_ref, vr2_ref.at[z], v2_send.at[q], v2_recv.at[z], device_id=dev, device_id_type=MESH)

    def v3_copy(e, dev):
        return pltpu.make_async_remote_copy(
            vs3_ref, vr3_ref.at[h], v3_send.at[e], v3_recv.at[h], device_id=dev, device_id_type=MESH)

    def v3_from(qh):
        return pltpu.make_async_remote_copy(
            vs3_ref, vr3_ref.at[qh], v3_send.at[0], v3_recv.at[qh],
            device_id={"col": 2 * qh + k, "grp": (2 * qh + k) * NZ + z}, device_id_type=MESH)

    vec_peer = {"col": c, "grp": c * NZ + z}

    def start_all(peer, copy, count):
        for d in range(count - 1):
            copy(*peer(d)).start()

    def wait_all(peer, src, dst_slots, send, recv, count):
        for d in range(count - 1):
            q, dev = peer(d)
            pltpu.make_async_remote_copy(
                src(q), dst_slots.at[q], send.at[q], recv.at[q], device_id=dev, device_id_type=MESH).wait_recv()

    def wait_sent(peer, copy, count):
        for d in range(count - 1):
            copy(*peer(d)).wait_send()

    start_all(plane_peer, h1_copy, NP)

    @pl.when(p != c)
    def _():
        v1_copy(vec_peer).start()

    @pl.when(p == c)
    def _():
        vr1_ref[p] = vs1_ref[...]

    hr1_ref[p] = hs1_ref[p]

    for t in range(tables):
        pg = mm_nt(pool_ref[t * width : (t + 1) * width], dpt_ref[...])
        half = NP // tables
        for q in range(half):
            ps1_ref[t * half + q] = pg[q * 128 : (q + 1) * 128].astype(BF)
    start_all(plane_peer, p1_copy, NP)
    pr1_ref[p] = ps1_ref[p]

    def row_grad(t):
        ws = slice(t * width, (t + 1) * width)
        dpool_ref[ws] = mm(wc_ref[ws], dpt_ref[...]).astype(BF)
        acc = mm_nt(cnts[0][t], dpool_ref[ws, :CH])
        for j in range(1, n_ch):
            acc = acc + mm_nt(cnts[j][t], dpool_ref[ws, j * CH : (j + 1) * CH])
        rg_ref[t] = acc
        pltpu.make_async_copy(rg_ref.at[t], rg_hbm.at[t], out_sem.at[t]).start()

    def slot_sum(ref, rows):
        acc = ref[0, rows].astype(F32)
        for q in range(1, NP):
            acc = acc + ref[q, rows].astype(F32)
        return acc

    row_grad(0)

    wait_all(plane_peer, lambda q: hs1_ref.at[q], hr1_ref, h1_send, h1_recv, NP)
    hs2_ref[...] = slot_sum(hr1_ref, slice(0, 32)).astype(BF)
    start_all(z_peer, h2_copy, NZ)
    hr2_ref[z] = hs2_ref[...]

    @pl.when(p == c)
    def _():
        wait_all(plane_peer, lambda q: vs1_ref, vr1_ref, v2_send, v1_recv, NP)
        vs2_ref[...] = slot_sum(vr1_ref, slice(0, 8))
        start_all(z_peer, v2_copy, NZ)
        vr2_ref[z] = vs2_ref[...]

    row_grad(1)

    wait_all(plane_peer, lambda q: ps1_ref.at[q], pr1_ref, p1_send, p1_recv, NP)
    for q in range(NZ):
        ps2_ref[q] = slot_sum(pr1_ref, slice(q * 16, (q + 1) * 16)).astype(BF)
    start_all(z_peer, p2_copy, NZ)
    pr2_ref[z] = ps2_ref[z]

    wait_all(z_peer, lambda q: hs2_ref, hr2_ref, h2_send, h2_recv, NZ)
    hs3_ref[...] = slot_sum(hr2_ref, slice(0, 32)).astype(BF)
    start_all(far_peer, h3_copy, 2 * NP)
    hr3_ref[h * NP + p] = hs3_ref[...]

    @pl.when(p == c)
    def _():
        wait_all(z_peer, lambda q: vs2_ref, vr2_ref, v2_send, v2_recv, NZ)
        vs3_ref[...] = slot_sum(vr2_ref, slice(0, 8))
        start_all(far_peer, v3_copy, 2 * NP)
        vr3_ref[h] = vs3_ref[...]

    row_grad(2)
    row_grad(3)

    wait_all(z_peer, lambda q: ps2_ref.at[q], pr2_ref, p2_send, p2_recv, NZ)
    proj_ref[...] = slot_sum(pr2_ref, slice(0, 16))
    proj_out = pltpu.make_async_copy(proj_ref, proj_hbm, out_sem.at[tables])
    proj_out.start()

    wait_all(far_peer, lambda e: hs3_ref, hr3_ref, h3_send, h3_recv, 2 * NP)
    h4 = pltpu.make_async_remote_copy(
        hr3_ref, hr_hbm.at[k], h4_send, h4_recv, device_id=core_peer, device_id_type=MESH)
    h4.start()
    hr_out = pltpu.make_async_copy(hr3_ref, hr_hbm.at[k], out_sem.at[tables + 1])
    hr_out.start()
    for qh in range(2):
        @pl.when((h != qh) | (p != c))
        def _():
            v3_from(qh).wait_recv()

    v4 = pltpu.make_async_remote_copy(
        vr3_ref, vec_hbm.at[k], v4_send, v4_recv, device_id=core_peer, device_id_type=MESH)
    v4.start()
    vec_out = pltpu.make_async_copy(vr3_ref, vec_hbm.at[k], out_sem.at[tables + 2])
    vec_out.start()

    for j in range(n_ch):
        copy_a(j).wait_send()
        copy_b(j).wait_send()
        copy_c(j).wait_send()
        for i in range(n_own):
            copy_n(j, i).wait_send()
    wait_sent(plane_peer, h1_copy, NP)
    wait_sent(plane_peer, p1_copy, NP)
    wait_sent(z_peer, h2_copy, NZ)
    wait_sent(z_peer, p2_copy, NZ)
    wait_sent(far_peer, h3_copy, 2 * NP)
    for t in range(tables):
        pltpu.make_async_copy(rg_ref.at[t], rg_hbm.at[t], out_sem.at[t]).wait()
    @pl.when(p != c)
    def _():
        v1_copy(vec_peer).wait_send()

    @pl.when(p == c)
    def _():
        wait_sent(z_peer, v2_copy, NZ)
        wait_sent(far_peer, v3_copy, 2 * NP)

    proj_out.wait()
    hr_out.wait()
    vec_out.wait()
    h4.wait_send()
    v4.wait_send()
    pltpu.make_async_remote_copy(
        hr3_ref, hr_hbm.at[1 - k], h4_send, h4_recv, device_id=core_peer, device_id_type=MESH).wait_recv()
    pltpu.make_async_remote_copy(
        vr3_ref, vec_hbm.at[1 - k], v4_send, v4_recv, device_id=core_peer, device_id_type=MESH).wait_recv()


def write_out(
    rg_hbm, proj_hbm, hr_hbm, vec_hbm, rg_out, proj_out, hid_out, bg_out, og_out,
    rg_ref, proj_ref, hr_ref, vec_ref, hid_ref, bg_ref, og_ref, in_sem, out_sem,
):
    tables = rg_ref.shape[0]

    def copy(src, dst, sem):
        return pltpu.make_async_copy(src, dst, sem)

    ins = [copy(hr_hbm, hr_ref, in_sem.at[0]), copy(vec_hbm, vec_ref, in_sem.at[1]), copy(proj_hbm, proj_ref, in_sem.at[2])]
    ins += [copy(rg_hbm.at[t], rg_ref.at[t], in_sem.at[3 + t]) for t in range(tables)]
    outs = [copy(rg_ref.at[t], rg_out.at[t], out_sem.at[t]) for t in range(tables)]
    outs += [
        copy(src, dst, out_sem.at[tables + n])
        for n, (src, dst) in enumerate(((proj_ref, proj_out), (hid_ref, hid_out), (bg_ref, bg_out), (og_ref, og_out)))
    ]
    for one in ins:
        one.start()
    for one in ins[:3]:
        one.wait()
    for core in range(2):
        for qh in range(2):
            col = slice((2 * qh + core) * 256, (2 * qh + core + 1) * 256)
            for q in range(NP):
                hid_ref[q * 32 : (q + 1) * 32, col] = hr_ref[core, qh * NP + q].astype(F32)
            bg_ref[:, col] = vec_ref[core, qh, 0:1]
            og_ref[:, col] = vec_ref[core, qh, 1:2]
    for one in outs[tables:]:
        one.start()
    for t in range(tables):
        ins[3 + t].wait()
        outs[t].start()
    for one in outs:
        one.wait()


def body(rows, bag_ids, bag_lengths, labels, proj_weight, hidden_weight, hidden_bias, out_weight):
    tables, row_total, width = rows.shape
    samples, _, bag = bag_ids.shape
    feats, proj = proj_weight.shape
    hid = hidden_weight.shape[1]
    own = tables * width
    n_ch = samples // CH
    ids = bag_ids.transpose(1, 2, 0)
    lens = bag_lengths.T
    hbm = pl.BlockSpec(memory_space=pl.ANY)
    dma = pltpu.SemaphoreType.DMA
    out = pl.pallas_call(
        kernel,
        out_shape=(
            jax.ShapeDtypeStruct(rows.shape, F32),
            jax.ShapeDtypeStruct((feats // 256, proj), F32),
            jax.ShapeDtypeStruct((2, 2 * NP, 32, 256), BF),
            jax.ShapeDtypeStruct((2, 2, 8, 256), F32),
        ),
        in_specs=[hbm] * 8,
        out_specs=[hbm] * 4,
        scratch_shapes=[
            pltpu.VMEM(rows.shape, F32),
            pltpu.VMEM((feats // 256, proj), F32),
            pltpu.VMEM((tables, bag, samples), jnp.int32),
            pltpu.VMEM((tables, samples), jnp.int32),
            pltpu.VMEM((1, samples), jnp.int32),
            pltpu.VMEM((proj, hid), BF),
            pltpu.VMEM((1, hid), F32),
            pltpu.VMEM((1, hid), F32),
            pltpu.VMEM((tables, bag, samples), jnp.int32),
            pltpu.VMEM((tables, row_total, width), F32),
            pltpu.VMEM((own, proj), BF),
            pltpu.VMEM((tables, 2 * width, row_total), BF),
            pltpu.VMEM((proj, own), BF),
            pltpu.VMEM((hid, proj), BF),
            pltpu.VMEM((hid, 128), F32),
            pltpu.VMEM((hid, 128), F32),
            *[pltpu.VMEM((tables, row_total, CH), BF)] * n_ch,
            pltpu.VMEM((own, samples), BF),
            pltpu.VMEM((n_ch, proj, CH), F32),
            pltpu.VMEM((n_ch, proj // 2, CH), F32),
            pltpu.VMEM((n_ch, proj // 2, CH), BF),
            pltpu.VMEM((n_ch, proj // 2, CH), BF),
            pltpu.VMEM((n_ch, proj, CH), BF),
            pltpu.VMEM((hid, samples), BF),
            pltpu.VMEM((proj + 16, 256), F32),
            pltpu.VMEM((16, 256), F32),
            pltpu.VMEM((proj, samples), BF),
            pltpu.VMEM((own, samples), BF),
            pltpu.VMEM((NP, 32, 256), BF),
            pltpu.VMEM((NP, 32, 256), BF),
            pltpu.VMEM((NP, 128, proj), BF),
            pltpu.VMEM((NP, 128, proj), BF),
            pltpu.VMEM((32, 256), BF),
            pltpu.VMEM((NZ, 32, 256), BF),
            pltpu.VMEM((NZ, 16, proj), BF),
            pltpu.VMEM((NZ, 16, proj), BF),
            pltpu.VMEM((32, 256), BF),
            pltpu.VMEM((2 * NP, 32, 256), BF),
            pltpu.VMEM((8, 256), F32),
            pltpu.VMEM((NP, 8, 256), F32),
            pltpu.VMEM((8, 256), F32),
            pltpu.VMEM((NZ, 8, 256), F32),
            pltpu.VMEM((8, 256), F32),
            pltpu.VMEM((2, 8, 256), F32),
            dma((tables + 7,)),
            dma((tables + 3,)),
            dma((n_ch * 2,)), dma((n_ch * 2,)),
            dma((n_ch,)), dma((n_ch,)), dma((n_ch,)), dma((n_ch,)), dma((n_ch,)), dma((n_ch,)),
            dma((NP,)), dma((NP,)), dma((NP,)), dma((NP,)),
            dma((NZ,)), dma((NZ,)), dma((NZ,)), dma((NZ,)),
            dma((2 * NP,)), dma((2 * NP,)),
            dma(()), dma(()),
            dma(()), dma((NP,)), dma((NZ,)), dma((NZ,)), dma((2 * NP,)), dma((2,)), dma(()), dma(()),
        ],
        compiler_params=pltpu.CompilerParams(
            collective_id=0, has_side_effects=True, vmem_limit_bytes=64 * 1024 * 1024
        ),
    )(
        ids, lens, labels.reshape(1, samples), hidden_weight, hidden_bias.reshape(1, hid),
        out_weight.reshape(1, hid), rows, proj_weight,
    )
    shapes = (
        jax.ShapeDtypeStruct(rows.shape, F32),
        jax.ShapeDtypeStruct((feats // 256, proj), F32),
        jax.ShapeDtypeStruct((proj, hid), F32),
        jax.ShapeDtypeStruct((1, hid), F32),
        jax.ShapeDtypeStruct((1, hid), F32),
    )
    held = [pltpu.VMEM(o.shape, o.dtype) for o in (*out, *shapes[2:])]
    out = pl.pallas_call(
        write_out,
        out_shape=shapes,
        in_specs=[hbm] * 4,
        out_specs=[hbm] * 5,
        scratch_shapes=held + [dma((tables + 3,)), dma((tables + 4,))],
        compiler_params=pltpu.CompilerParams(vmem_limit_bytes=64 * 1024 * 1024),
    )(*out)
    return out[0], out[1], out[2], out[3].reshape(hid), out[4].reshape(hid)


def solution(mesh):
    return jax.shard_map(
        body,
        mesh=mesh,
        in_specs=(
            P(None, "grp", "col"),
            P("grp", None, None),
            P("grp", None),
            P("grp"),
            P(),
            P(),
            P(),
            P(),
        ),
        out_specs=(P(None, "grp", "col"), P(("col", "grp"), None), P(), P(), P()),
        check_vma=False,
    )
```
